32 devices in a mesh: groups: 2 (over x), tm: 16 (over z, y, core).
Axes of the slice: x: 2, y: 2, z: 4, core: 2. Of those that a mesh axis runs over, the one named last changes fastest.
Arguments:
- trans_matrix: bfloat16 [1024, 1024], replicated, may hold values from -1 to 1
- ensemble: bfloat16 [1024, 128], replicated, may hold values from -16 to 16
- obs_operator: bfloat16 [32, 256, 256], P(('groups', 'tm')), parts along dimension 0, may hold values from -0.375 to 0.375
- pattern: int32 [32, 2, 2], P(('groups', 'tm')), parts along dimension 0, may hold values from 0 to 7, as said below
- counts: int32 [32], P(('groups', 'tm')), parts along dimension 0, may hold values from 64 to 256, as said below
- observations: float32 [32, 256], P(('groups', 'tm')), parts along dimension 0, may hold values from -6 to 6
- obs_variance: float32 [32, 256], P(('groups', 'tm')), parts along dimension 0, may hold values from 0.04 to 8
- initial_state: float32 [2048], P('groups'), parts along dimension 0, may hold values from -6 to 6
Outputs:
- states: float32 [32, 1024], P(('groups', 'tm')), parts along dimension 0
- misfit: float32 [2], P('groups'), parts along dimension 0
The draws below stay inside these ranges and needn't reach their ends.
There are 2 independent parts, one for each index of `groups`. The reference program is written for one: setup_inputs(seed, part) draws one part's arguments, and reference() takes and returns one part's arrays. A program takes and returns all parts, laid end to end along the dimension named above; an argument that names none is the same for every part. Nothing has to cross between parts.
Inputs may be any that keep to these rules, and one draw needn't show every extreme that they name: `pattern`: the 2 entries of a row name different blocks. `counts`: some step has all 256 rows live.
All inputs are finite; a program needn't handle non-finite values.
Results may differ from the reference program's by a relative error of at most 0.02.
Values may be sent and summed in bfloat16 or wider, within the bound.
A program may use at most 512 MiB of HBM per device.

```python
import math
import jax
import jax.numpy as jnp
from jax import lax

N = 1024
BLK = 128
NB = 8
MB = 2
KB = 2
MOBS = 256
NE = 128
TIME = 16


def draw_trans_matrix(key, part):
    key = jax.random.fold_in(key, 11)
    first, second = jax.random.split(key)
    diagonal = jax.random.uniform(first, (N,), jnp.float32, 0.7, 0.8)
    spread = jax.random.normal(second, (N, N), jnp.float32) * (0.22 / math.sqrt(N))
    unit = jnp.eye(N, dtype=jnp.float32)
    return (spread * (1.0 - unit) + unit * diagonal[:, None]).astype(jnp.bfloat16)


def draw_ensemble(key, part):
    key = jax.random.fold_in(key, 41)
    values = jnp.clip(jax.random.normal(key, (N, NE), jnp.float32) * 4.0, -16.0, 16.0)
    return values.astype(jnp.bfloat16)


def draw_obs_variance(key, part):
    key = jax.random.fold_in(key, 53)
    first = jax.random.fold_in(key, 0)
    logs = jax.random.uniform(first, (TIME, MOBS), jnp.float32, math.log(0.04), math.log(8.0))
    return jnp.clip(jnp.exp(logs), 0.04, 8.0).astype(jnp.float32)


def draw_pattern(key, part):
    key = jax.random.fold_in(key, 23)
    subkeys = jax.random.split(key, TIME * MB)
    chosen = jax.vmap(lambda single: jax.random.permutation(single, NB)[:KB])(subkeys)
    return chosen.reshape(TIME, MB, KB).astype(jnp.int32)


def draw_counts(key, part):
    key = jax.random.fold_in(key, 37)
    first, second = jax.random.split(key)
    values = jax.random.randint(first, (TIME,), MOBS // 4, MOBS + 1, dtype=jnp.int32)
    placed = jax.random.randint(second, (), 0, TIME, dtype=jnp.int32)
    return values.at[placed].set(MOBS)


def level_of(stream_key, shape, pieces, least, top_value):
    def one(dim, blocks):
        draws = jax.random.uniform(jax.random.fold_in(jax.random.fold_in(stream_key, 6), dim), (blocks,), jnp.float32, least / len(pieces), top_value / len(pieces))
        return jnp.repeat(jnp.exp(draws), shape[dim] // blocks).reshape((-1,) + (1,) * (len(shape) - dim - 1))

    factor_of = one(*pieces[0])
    for cut in pieces[1:]:
        factor_of = factor_of * one(*cut)
    return factor_of


def bell_draw(key, shape, scale, bound, shards=(), held_as=jnp.bfloat16):
    gain = level_of(key, shape, shards, -0.22, 0.18) if shards else 1.0
    array = jax.random.normal(key, shape, jnp.float32) * scale * gain
    return jnp.minimum(jnp.maximum(array, -bound), bound).astype(held_as)


def setup_inputs(seed: int = 0, part: int = 0) -> dict:
    key_of = jax.random.split(jax.random.key(seed), 9)
    own_keys = jax.random.split(jax.random.fold_in(key_of[8], part), 9)
    return {
        "trans_matrix": draw_trans_matrix(jax.random.fold_in(key_of[8], 71), part),
        "ensemble": draw_ensemble(jax.random.fold_in(key_of[8], 71), part),
        "obs_operator": bell_draw(own_keys[2], (TIME, MOBS, KB * BLK), (KB * BLK) ** -0.5, 0.375, ((0, 16),)),
        "pattern": draw_pattern(jax.random.fold_in(jax.random.fold_in(key_of[8], part), 71), part),
        "counts": draw_counts(jax.random.fold_in(jax.random.fold_in(key_of[8], part), 71), part),
        "observations": bell_draw(own_keys[5], (TIME, MOBS), 1.0, 6.0, ((0, 16),), jnp.float32),
        "obs_variance": draw_obs_variance(jax.random.fold_in(jax.random.fold_in(key_of[8], part), 71), part),
        "initial_state": bell_draw(own_keys[7], (N,), 1.0, 6.0, (), jnp.float32),
    }


def element_maps(trans_matrix, ensemble, hrows, cols, count, yobs, rvar):
    fcols = trans_matrix.reshape(NB, BLK, N)[cols].reshape(MB, KB * BLK, N)
    ecols = ensemble.reshape(NB, BLK, NE)[cols].reshape(MB, KB * BLK, NE)
    hblock = hrows.reshape(MB, BLK, KB * BLK).astype(jnp.float32)
    active_rows = (jnp.arange(MOBS, dtype=jnp.int32) < count).astype(jnp.float32)
    forward = jnp.einsum('mrk,mkn->mrn', hblock, fcols.astype(jnp.float32)).reshape(MOBS, N) * active_rows[:, None]
    member = jnp.einsum('mrk,mkn->mrn', hblock, ecols.astype(jnp.float32)).reshape(MOBS, NE) * active_rows[:, None]
    covariance = jnp.dot(member, member.T, precision=lax.Precision.HIGHEST) / NE + jnp.diag(rvar)
    factor = jnp.linalg.cholesky(covariance)
    solved = jax.scipy.linalg.cho_solve((factor, True), member)
    masked_obs = yobs * active_rows
    reduced = (jnp.dot(solved.T, forward, precision=lax.Precision.HIGHEST) / NE).astype(jnp.bfloat16)
    transit = (trans_matrix.astype(jnp.float32) - jnp.dot(ensemble.astype(jnp.float32), reduced.astype(jnp.float32), preferred_element_type=jnp.float32)).astype(jnp.bfloat16)
    weights = jnp.dot(solved.T, masked_obs, precision=lax.Precision.HIGHEST) / NE
    offset = jnp.dot(ensemble.astype(jnp.float32), weights, precision=lax.Precision.HIGHEST)
    return (transit, offset, forward, factor, masked_obs)

def reference(trans_matrix, ensemble, obs_operator, pattern, counts, observations, obs_variance, initial_state):

    def advance_step(carried, inputs):
        hrows, cols, count, yobs, rvar = inputs
        transit, offset, forward, factor, masked_obs = element_maps(trans_matrix, ensemble, hrows, cols, count, yobs, rvar)
        innovation = masked_obs - jnp.dot(forward, carried, precision=lax.Precision.HIGHEST)
        quadratic = jnp.sum(innovation * jax.scipy.linalg.cho_solve((factor, True), innovation))
        produced = jnp.dot(transit.astype(jnp.float32), carried, precision=lax.Precision.HIGHEST) + offset
        return (produced, (produced, quadratic))
    final_state, outputs = lax.scan(advance_step, initial_state, (obs_operator, pattern, counts, observations, obs_variance))
    states, quadratic = outputs
    misfit = jnp.sum(quadratic) / jnp.sum(counts.astype(jnp.float32))
    return (states, misfit.reshape(1))
```

```python
import functools

import jax
import jax.numpy as jnp
from jax import lax
from jax.experimental import pallas as pl
from jax.experimental.pallas import tpu as pltpu
from jax.sharding import PartitionSpec as P

N = 1024
BLK = 128
NB = 8
MB = 2
KB = 2
MOBS = 256
NE = 128
HIGH = lax.Precision.HIGHEST
VMEM = pl.BlockSpec(memory_space=pltpu.VMEM)
SMEM = pl.BlockSpec(memory_space=pltpu.SMEM)


def times(left, right, precision=None):
    return lax.dot_general(
        left, right, (((1,), (0,)), ((), ())), precision=precision, preferred_element_type=jnp.float32
    )


def times_t(left, right, precision=None):
    return lax.dot_general(
        left, right, (((1,), (1,)), ((), ())), precision=precision, preferred_element_type=jnp.float32
    )


def maps_kernel(
    pattern, count, trans, ensemble, hrows, yobs, rvar,
    transit, offset, forward, gain, member, dinv, masked, swept,
):
    live = count[0]
    rows = lax.broadcasted_iota(jnp.int32, (MOBS, 1), 0)
    active_rows = (rows < live).astype(jnp.float32)
    lanes = lax.broadcasted_iota(jnp.int32, (1, MOBS), 1)
    active_lanes = (lanes < live).astype(jnp.float32)
    for m in range(MB):
        here = pl.ds(m * BLK, BLK)
        starts = [pl.multiple_of(pattern[0, m, k] * BLK, BLK) for k in range(KB)]
        hblock = hrows[0, here, :]
        ecols = jnp.concatenate([ensemble[pl.ds(s, BLK), :] for s in starts], axis=0)
        fcols = jnp.concatenate([trans[pl.ds(s, BLK), :] for s in starts], axis=0)
        alive = active_rows[m * BLK : (m + 1) * BLK]
        member[here, :] = times(hblock, ecols) * alive
        forward[here, :] = times(hblock, fcols) * alive
    inverse_var = active_lanes / rvar[...]
    dinv[...] = inverse_var
    masked[...] = yobs[...] * active_lanes
    scaled = member[...].T * inverse_var
    row = lax.broadcasted_iota(jnp.int32, (NE, NE), 0)
    lane = lax.broadcasted_iota(jnp.int32, (NE, NE), 1)
    start = times(scaled, member[...], HIGH) / NE + (row == lane).astype(jnp.float32)
    swept[...] = (start + start.T) * 0.5

    def sweep(k, carry):
        x = swept[...]
        r = swept[pl.ds(k, 1), :]
        on_lane = lane == k
        on_row = row == k
        c = jnp.sum(jnp.where(on_lane, x, 0.0), axis=1, keepdims=True)
        one_lane = lax.broadcasted_iota(jnp.int32, (1, NE), 1) == k
        pivot = jnp.sum(jnp.where(one_lane, r, 0.0), axis=1, keepdims=True)
        inv = 1.0 / pivot
        scaled_r = jnp.where(one_lane, -inv, r * inv)
        out = jnp.where(on_lane, c * inv, x - c * scaled_r)
        swept[...] = jnp.where(on_row, scaled_r, out)
        return carry

    lax.fori_loop(0, NE, sweep, 0)
    gains = times(-swept[...], scaled, HIGH) / NE
    gain[...] = gains
    reduced = times(gains, forward[...], HIGH).astype(jnp.bfloat16)
    transit[...] = (trans[...].astype(jnp.float32) - times(ensemble[...], reduced)).astype(
        jnp.bfloat16
    )
    seen = jnp.broadcast_to(masked[...], (8, MOBS))
    weights = times_t(seen, gains, HIGH)
    offset[...] = times_t(weights, ensemble[...].astype(jnp.float32), HIGH)[:1]


def split_rows(vector):
    high = vector.astype(jnp.bfloat16).astype(jnp.float32)
    rest = vector - high
    middle = rest.astype(jnp.bfloat16).astype(jnp.float32)
    lowest = rest - middle
    row = lax.broadcasted_iota(jnp.int32, (16, N), 0)
    stacked = jnp.where(row == 0, high, jnp.where(row == 1, middle, jnp.where(row == 2, lowest, 0.0)))
    return stacked.astype(jnp.bfloat16)


def chain_kernel(
    n, count, transit, offset, forward, gain, member, dinv, masked, first,
    states, misfit,
    incoming, current, produced, tiles, send_sem, recv_sem, tile_send, tile_recv,
):
    me = lax.axis_index("tm")
    barrier = pltpu.get_barrier_semaphore()

    def greet(i, carry):
        pl.semaphore_signal(barrier, inc=1, device_id={"tm": lax.rem(me + i, n)})
        return carry

    lax.fori_loop(1, n, greet, 0)
    pl.semaphore_wait(barrier, n - 1)

    pass_on = pltpu.make_async_remote_copy(
        src_ref=produced,
        dst_ref=incoming,
        send_sem=send_sem,
        recv_sem=recv_sem,
        device_id={"tm": lax.rem(me + 1, n)},
    )

    @pl.when(me == 0)
    def _():
        current[...] = first[...]

    @pl.when(me > 0)
    def _():
        pass_on.wait_recv()
        current[...] = incoming[...]

    before = current[...]
    parts = times_t(split_rows(before), transit[...])
    after = jnp.sum(parts, axis=0, keepdims=True) + offset[...]
    produced[...] = after

    @pl.when(me < n - 1)
    def _():
        pass_on.start()

    states[...] = after
    innovation = jnp.broadcast_to(masked[...], (8, MOBS)) - times_t(
        jnp.broadcast_to(before, (8, N)), forward[...], HIGH
    )
    moved = times_t(innovation, gain[...], HIGH)
    left = innovation - times_t(moved, member[...], HIGH)
    fit = jnp.sum(left * left * dinv[...], axis=1, keepdims=True) + NE * jnp.sum(
        moved * moved, axis=1, keepdims=True
    )
    lane = lax.broadcasted_iota(jnp.int32, (8, NE), 1)
    live = count[0].astype(jnp.float32)
    tiles[me] = jnp.where(lane == 0, fit, live)

    def tell(i):
        return pltpu.make_async_remote_copy(
            src_ref=tiles.at[me],
            dst_ref=tiles.at[me],
            send_sem=tile_send.at[i],
            recv_sem=tile_recv.at[me],
            device_id={"tm": lax.rem(me + i, n)},
        )

    def hear(i):
        other = lax.rem(me + n - i, n)
        return pltpu.make_async_remote_copy(
            src_ref=tiles.at[other],
            dst_ref=tiles.at[other],
            send_sem=tile_send.at[i],
            recv_sem=tile_recv.at[other],
            device_id={"tm": other},
        )

    def start(i, carry):
        tell(i).start()
        return carry

    def finish(i, carry):
        hear(i).wait_recv()
        return carry

    def sent(i, carry):
        tell(i).wait_send()
        return carry

    lax.fori_loop(1, n, start, 0)
    lax.fori_loop(1, n, finish, 0)
    lax.fori_loop(1, n, sent, 0)

    @pl.when(me < n - 1)
    def _():
        pass_on.wait_send()

    total = jnp.sum(tiles[...], axis=0)[:1]
    one = lax.broadcasted_iota(jnp.int32, (1, NE), 1)
    fits = jnp.sum(jnp.where(one == 0, total, 0.0), axis=1, keepdims=True)
    lives = jnp.sum(jnp.where(one == 1, total, 0.0), axis=1, keepdims=True)
    misfit[...] = jnp.broadcast_to(fits / lives, (1, NE))


def shards(
    n, trans_matrix, ensemble, obs_operator, pattern, counts, observations, obs_variance, initial_state
):
    f32 = jnp.float32
    transit, offset, forward, gain, member, dinv, masked = pl.pallas_call(
        maps_kernel,
        out_shape=(
            jax.ShapeDtypeStruct((N, N), jnp.bfloat16),
            jax.ShapeDtypeStruct((1, N), f32),
            jax.ShapeDtypeStruct((MOBS, N), f32),
            jax.ShapeDtypeStruct((NE, MOBS), f32),
            jax.ShapeDtypeStruct((MOBS, NE), f32),
            jax.ShapeDtypeStruct((1, MOBS), f32),
            jax.ShapeDtypeStruct((1, MOBS), f32),
        ),
        in_specs=[SMEM, SMEM] + [VMEM] * 5,
        out_specs=(VMEM,) * 7,
        scratch_shapes=[pltpu.VMEM((NE, NE), f32)],
        compiler_params=pltpu.CompilerParams(vmem_limit_bytes=48 * 1024 * 1024),
        name="maps",
    )(pattern, counts, trans_matrix, ensemble, obs_operator, observations, obs_variance)
    states, misfit = pl.pallas_call(
        functools.partial(chain_kernel, n),
        out_shape=(jax.ShapeDtypeStruct((1, N), f32), jax.ShapeDtypeStruct((1, NE), f32)),
        in_specs=[SMEM] + [VMEM] * 8,
        out_specs=(VMEM, VMEM),
        scratch_shapes=[
            pltpu.VMEM((1, N), f32),
            pltpu.VMEM((1, N), f32),
            pltpu.VMEM((1, N), f32),
            pltpu.VMEM((n, 8, NE), f32),
            pltpu.SemaphoreType.DMA,
            pltpu.SemaphoreType.DMA,
            pltpu.SemaphoreType.DMA((n,)),
            pltpu.SemaphoreType.DMA((n,)),
        ],
        compiler_params=pltpu.CompilerParams(
            collective_id=0, has_side_effects=True, vmem_limit_bytes=48 * 1024 * 1024
        ),
        name="chain",
    )(counts, transit, offset, forward, gain, member, dinv, masked, initial_state.reshape(1, N))
    return states, misfit[0, :1]


def solution(mesh):
    return jax.shard_map(
        functools.partial(shards, mesh.shape["tm"]),
        mesh=mesh,
        in_specs=(
            P(),
            P(),
            P(("groups", "tm"), None, None),
            P(("groups", "tm"), None, None),
            P(("groups", "tm")),
            P(("groups", "tm"), None),
            P(("groups", "tm"), None),
            P("groups"),
        ),
        out_specs=(P(("groups", "tm"), None), P("groups")),
        check_vma=False,
    )
```

```python
import functools

import jax
import jax.numpy as jnp
from jax import lax
from jax.experimental import pallas as pl
from jax.experimental.pallas import tpu as pltpu
from jax.sharding import PartitionSpec as P

N = 1024
BLK = 128
NB = 8
MB = 2
KB = 2
MOBS = 256
NE = 128
HIGH = lax.Precision.HIGHEST
VMEM = pl.BlockSpec(memory_space=pltpu.VMEM)
SMEM = pl.BlockSpec(memory_space=pltpu.SMEM)


def times(left, right, precision=None):
    return lax.dot_general(
        left, right, (((1,), (0,)), ((), ())), precision=precision, preferred_element_type=jnp.float32
    )


def times_t(left, right, precision=None):
    return lax.dot_general(
        left, right, (((1,), (1,)), ((), ())), precision=precision, preferred_element_type=jnp.float32
    )


def split_rows(vector):
    high = vector.astype(jnp.bfloat16).astype(jnp.float32)
    rest = vector - high
    middle = rest.astype(jnp.bfloat16).astype(jnp.float32)
    lowest = rest - middle
    row = lax.broadcasted_iota(jnp.int32, (16, N), 0)
    stacked = jnp.where(row == 0, high, jnp.where(row == 1, middle, jnp.where(row == 2, lowest, 0.0)))
    return stacked.astype(jnp.bfloat16)


def apply_rows(matrix, vector):
    return jnp.sum(times_t(split_rows(vector), matrix), axis=0, keepdims=True)


def observe_kernel(
    pattern, count, trans_hbm, ensemble, hrows, yobs, rvar,
    reduced, offset, forward, gain, member, dinv_out, masked_out,
    trans, swept, trans_sem,
):
    fetch = pltpu.make_async_copy(trans_hbm, trans, trans_sem)
    fetch.start()
    live = count[0]
    rows = lax.broadcasted_iota(jnp.int32, (MOBS, 1), 0)
    active_rows = (rows < live).astype(jnp.float32)
    lanes = lax.broadcasted_iota(jnp.int32, (1, MOBS), 1)
    active_lanes = (lanes < live).astype(jnp.float32)
    for m in range(MB):
        here = pl.ds(m * BLK, BLK)
        starts = [pl.multiple_of(pattern[0, m, k] * BLK, BLK) for k in range(KB)]
        ecols = jnp.concatenate([ensemble[pl.ds(s, BLK), :] for s in starts], axis=0)
        alive = active_rows[m * BLK : (m + 1) * BLK]
        member[here, :] = times(hrows[0, here, :], ecols) * alive
    dinv = active_lanes / rvar[...]
    masked = yobs[...] * active_lanes
    scaled = member[...].T * dinv
    row = lax.broadcasted_iota(jnp.int32, (NE, NE), 0)
    lane = lax.broadcasted_iota(jnp.int32, (NE, NE), 1)
    begin = times(scaled, member[...], HIGH) / NE + (row == lane).astype(jnp.float32)
    swept[...] = (begin + begin.T) * 0.5

    def sweep(k, carry):
        x = swept[...]
        r = swept[pl.ds(k, 1), :]
        on_lane = lane == k
        on_row = row == k
        c = jnp.sum(jnp.where(on_lane, x, 0.0), axis=1, keepdims=True)
        one_lane = lax.broadcasted_iota(jnp.int32, (1, NE), 1) == k
        pivot = jnp.sum(jnp.where(one_lane, r, 0.0), axis=1, keepdims=True)
        inv = 1.0 / pivot
        scaled_r = jnp.where(one_lane, -inv, r * inv)
        out = jnp.where(on_lane, c * inv, x - c * scaled_r)
        swept[...] = jnp.where(on_row, scaled_r, out)
        return carry

    lax.fori_loop(0, NE, sweep, 0)
    gains = times(-swept[...], scaled, HIGH) / NE
    seen = jnp.broadcast_to(masked, (8, MOBS))
    weights = times_t(seen, gains, HIGH)
    gain[...] = gains
    dinv_out[...] = dinv
    masked_out[...] = masked
    offset[...] = times_t(weights, ensemble[...].astype(jnp.float32), HIGH)[:1]

    fetch.wait()
    for m in range(MB):
        here = pl.ds(m * BLK, BLK)
        starts = [pl.multiple_of(pattern[0, m, k] * BLK, BLK) for k in range(KB)]
        fcols = jnp.concatenate([trans[pl.ds(s, BLK), :] for s in starts], axis=0)
        alive = active_rows[m * BLK : (m + 1) * BLK]
        forward[here, :] = times(hrows[0, here, :], fcols) * alive
    reduced[...] = times(gains, forward[...], HIGH).astype(jnp.bfloat16)


def chain_kernel(
    n, count, trans_hbm, ensemble, reduced, offset, forward, gain, member, dinv_in, masked, first,
    states, misfit,
    trans, transit, earlier, step, reduced_in,
    offset_in, step_offset, incoming, current, produced, tiles,
    trans_sem, pair_send, pair_recv, hop_send, hop_recv, tile_send, tile_recv,
):
    me = lax.axis_index("tm")
    odd = lax.rem(me, 2) == 1
    even = lax.rem(me, 2) == 0
    fetch = pltpu.make_async_copy(trans_hbm, trans, trans_sem)
    fetch.start()
    barrier = pltpu.get_barrier_semaphore()

    def greet(i, carry):
        pl.semaphore_signal(barrier, inc=1, device_id={"tm": lax.rem(me + i, n)})
        return carry

    lax.fori_loop(1, n, greet, 0)
    pl.semaphore_wait(barrier, n - 1)
    after_me = lax.rem(me + 1, n)
    after_that = lax.rem(me + 2, n)
    give_matrix = pltpu.make_async_remote_copy(
        src_ref=reduced, dst_ref=reduced_in, send_sem=pair_send.at[0], recv_sem=pair_recv.at[0],
        device_id={"tm": after_me},
    )
    give_offset = pltpu.make_async_remote_copy(
        src_ref=offset, dst_ref=offset_in, send_sem=pair_send.at[1], recv_sem=pair_recv.at[1],
        device_id={"tm": after_me},
    )
    far = pltpu.make_async_remote_copy(
        src_ref=produced, dst_ref=incoming, send_sem=hop_send.at[0], recv_sem=hop_recv,
        device_id={"tm": after_that},
    )
    near = pltpu.make_async_remote_copy(
        src_ref=produced, dst_ref=incoming, send_sem=hop_send.at[1], recv_sem=hop_recv,
        device_id={"tm": after_me},
    )

    @pl.when(even)
    def _():
        give_matrix.start()
        give_offset.start()

    fetch.wait()

    def transit_of(low_rank):
        return (trans[...].astype(jnp.float32) - times(ensemble[...], low_rank)).astype(jnp.bfloat16)

    @pl.when(even)
    def _():
        step[...] = transit_of(reduced[...])
        step_offset[...] = offset[...]

    @pl.when(odd)
    def _():
        transit[...] = transit_of(reduced[...])
        give_matrix.wait_recv()
        give_offset.wait_recv()
        earlier[...] = transit_of(reduced_in[...])

        def product(i, carry):
            columns = pl.ds(pl.multiple_of(i * 256, 256), 256)
            step[:, columns] = times(transit[...], earlier[:, columns]).astype(jnp.bfloat16)
            return carry

        lax.fori_loop(0, N // 256, product, 0)
        step_offset[...] = apply_rows(transit[...], offset_in[...]) + offset[...]

    @pl.when(me < 2)
    def _():
        current[...] = first[...]

    @pl.when(me >= 2)
    def _():
        near.wait_recv()
        current[...] = incoming[...]

    produced[...] = apply_rows(step[...], current[...]) + step_offset[...]
    sends = jnp.logical_and(odd, me < n - 1)

    @pl.when(sends)
    def _():
        far.start()
        near.start()

    states[...] = produced[...]

    @pl.when(odd)
    def _():
        current[...] = apply_rows(earlier[...], current[...]) + offset_in[...]

    seen = jnp.broadcast_to(masked[...], (8, MOBS))
    innovation = seen - times_t(jnp.broadcast_to(current[...], (8, N)), forward[...], HIGH)
    moved = times_t(innovation, gain[...], HIGH)
    left = innovation - times_t(moved, member[...], HIGH)
    fit = jnp.sum(left * left * dinv_in[...], axis=1, keepdims=True) + NE * jnp.sum(
        moved * moved, axis=1, keepdims=True
    )
    tile_lane = lax.broadcasted_iota(jnp.int32, (8, NE), 1)
    tiles[me] = jnp.where(tile_lane == 0, fit, count[0].astype(jnp.float32))

    def tell(i):
        return pltpu.make_async_remote_copy(
            src_ref=tiles.at[me],
            dst_ref=tiles.at[me],
            send_sem=tile_send.at[i],
            recv_sem=tile_recv.at[me],
            device_id={"tm": lax.rem(me + i, n)},
        )

    def hear(i):
        other = lax.rem(me + n - i, n)
        return pltpu.make_async_remote_copy(
            src_ref=tiles.at[other],
            dst_ref=tiles.at[other],
            send_sem=tile_send.at[i],
            recv_sem=tile_recv.at[other],
            device_id={"tm": other},
        )

    def start(i, carry):
        tell(i).start()
        return carry

    def finish(i, carry):
        hear(i).wait_recv()
        return carry

    def sent(i, carry):
        tell(i).wait_send()
        return carry

    lax.fori_loop(1, n, start, 0)
    lax.fori_loop(1, n, finish, 0)
    lax.fori_loop(1, n, sent, 0)

    @pl.when(even)
    def _():
        give_matrix.wait_send()
        give_offset.wait_send()

    @pl.when(sends)
    def _():
        far.wait_send()
        near.wait_send()

    total = jnp.sum(tiles[...], axis=0)[:1]
    one = lax.broadcasted_iota(jnp.int32, (1, NE), 1)
    fits = jnp.sum(jnp.where(one == 0, total, 0.0), axis=1, keepdims=True)
    lives = jnp.sum(jnp.where(one == 1, total, 0.0), axis=1, keepdims=True)
    misfit[...] = jnp.broadcast_to(fits / lives, (1, NE))


def shards(
    n, trans_matrix, ensemble, obs_operator, pattern, counts, observations, obs_variance, initial_state
):
    f32, bf16 = jnp.float32, jnp.bfloat16
    hbm = pl.BlockSpec(memory_space=pltpu.HBM)
    observed = pl.pallas_call(
        observe_kernel,
        out_shape=(
            jax.ShapeDtypeStruct((NE, N), bf16),
            jax.ShapeDtypeStruct((1, N), f32),
            jax.ShapeDtypeStruct((MOBS, N), f32),
            jax.ShapeDtypeStruct((NE, MOBS), f32),
            jax.ShapeDtypeStruct((MOBS, NE), f32),
            jax.ShapeDtypeStruct((1, MOBS), f32),
            jax.ShapeDtypeStruct((1, MOBS), f32),
        ),
        in_specs=[SMEM, SMEM, hbm] + [VMEM] * 4,
        out_specs=(VMEM,) * 7,
        scratch_shapes=[
            pltpu.VMEM((N, N), bf16),
            pltpu.VMEM((NE, NE), f32),
            pltpu.SemaphoreType.DMA,
        ],
        compiler_params=pltpu.CompilerParams(vmem_limit_bytes=32 * 1024 * 1024),
        name="observe",
    )(pattern, counts, trans_matrix, ensemble, obs_operator, observations, obs_variance)
    states, misfit = pl.pallas_call(
        functools.partial(chain_kernel, n),
        out_shape=(jax.ShapeDtypeStruct((1, N), f32), jax.ShapeDtypeStruct((1, NE), f32)),
        in_specs=[SMEM, hbm] + [VMEM] * 9,
        out_specs=(VMEM, VMEM),
        scratch_shapes=[
            pltpu.VMEM((N, N), bf16),
            pltpu.VMEM((N, N), bf16),
            pltpu.VMEM((N, N), bf16),
            pltpu.VMEM((N, N), bf16),
            pltpu.VMEM((NE, N), bf16),
            pltpu.VMEM((1, N), f32),
            pltpu.VMEM((1, N), f32),
            pltpu.VMEM((1, N), f32),
            pltpu.VMEM((1, N), f32),
            pltpu.VMEM((1, N), f32),
            pltpu.VMEM((n, 8, NE), f32),
            pltpu.SemaphoreType.DMA,
            pltpu.SemaphoreType.DMA((2,)),
            pltpu.SemaphoreType.DMA((2,)),
            pltpu.SemaphoreType.DMA((2,)),
            pltpu.SemaphoreType.DMA,
            pltpu.SemaphoreType.DMA((n,)),
            pltpu.SemaphoreType.DMA((n,)),
        ],
        compiler_params=pltpu.CompilerParams(
            collective_id=0, has_side_effects=True, vmem_limit_bytes=40 * 1024 * 1024
        ),
        name="chain",
    )(counts, trans_matrix, ensemble, *observed, initial_state.reshape(1, N))
    return states, misfit[0, :1]


def solution(mesh):
    return jax.shard_map(
        functools.partial(shards, mesh.shape["tm"]),
        mesh=mesh,
        in_specs=(
            P(),
            P(),
            P(("groups", "tm"), None, None),
            P(("groups", "tm"), None, None),
            P(("groups", "tm")),
            P(("groups", "tm"), None),
            P(("groups", "tm"), None),
            P("groups"),
        ),
        out_specs=(P(("groups", "tm"), None), P("groups")),
        check_vma=False,
    )
```

```python
import functools

import jax
import jax.numpy as jnp
from jax import lax
from jax.experimental import pallas as pl
from jax.experimental.pallas import tpu as pltpu
from jax.sharding import PartitionSpec as P

N = 1024
BLK = 128
NB = 8
MB = 2
KB = 2
MOBS = 256
NE = 128
HIGH = lax.Precision.HIGHEST
VMEM = pl.BlockSpec(memory_space=pltpu.VMEM)
SMEM = pl.BlockSpec(memory_space=pltpu.SMEM)


def times(left, right, precision=None):
    return lax.dot_general(
        left, right, (((1,), (0,)), ((), ())), precision=precision, preferred_element_type=jnp.float32
    )


def times_t(left, right, precision=None):
    return lax.dot_general(
        left, right, (((1,), (1,)), ((), ())), precision=precision, preferred_element_type=jnp.float32
    )


def split_rows(vector):
    high = vector.astype(jnp.bfloat16).astype(jnp.float32)
    rest = vector - high
    middle = rest.astype(jnp.bfloat16).astype(jnp.float32)
    lowest = rest - middle
    row = lax.broadcasted_iota(jnp.int32, (16, N), 0)
    stacked = jnp.where(row == 0, high, jnp.where(row == 1, middle, jnp.where(row == 2, lowest, 0.0)))
    return stacked.astype(jnp.bfloat16)


def apply_rows(matrix, vector):
    return jnp.sum(times_t(split_rows(vector), matrix), axis=0, keepdims=True)


def observe_kernel(
    pattern, count, trans_hbm, ensemble, hrows, yobs, rvar,
    reduced, offset, forward, gain, member, dinv_out, masked_out,
    trans, swept, trans_sem,
):
    fetch = pltpu.make_async_copy(trans_hbm, trans, trans_sem)
    fetch.start()
    live = count[0]
    rows = lax.broadcasted_iota(jnp.int32, (MOBS, 1), 0)
    active_rows = (rows < live).astype(jnp.float32)
    lanes = lax.broadcasted_iota(jnp.int32, (1, MOBS), 1)
    active_lanes = (lanes < live).astype(jnp.float32)
    for m in range(MB):
        here = pl.ds(m * BLK, BLK)
        starts = [pl.multiple_of(pattern[0, m, k] * BLK, BLK) for k in range(KB)]
        ecols = jnp.concatenate([ensemble[pl.ds(s, BLK), :] for s in starts], axis=0)
        alive = active_rows[m * BLK : (m + 1) * BLK]
        member[here, :] = times(hrows[0, here, :], ecols) * alive
    dinv = active_lanes / rvar[...]
    masked = yobs[...] * active_lanes
    scaled = member[...].T * dinv
    row = lax.broadcasted_iota(jnp.int32, (NE, NE), 0)
    lane = lax.broadcasted_iota(jnp.int32, (NE, NE), 1)
    begin = times(scaled, member[...], HIGH) / NE + (row == lane).astype(jnp.float32)
    swept[...] = (begin + begin.T) * 0.5

    one_lane = lax.broadcasted_iota(jnp.int32, (1, NE), 1)

    def pick(vector, k):
        return jnp.sum(jnp.where(one_lane == k, vector, 0.0), axis=1, keepdims=True)

    def sweep(j, carry):
        k = 2 * j
        x = swept[...]
        r0 = swept[pl.ds(k, 1), :]
        r1 = swept[pl.ds(k + 1, 1), :]
        c0 = jnp.sum(jnp.where(lane == k, x, 0.0), axis=1, keepdims=True)
        c1 = jnp.sum(jnp.where(lane == k + 1, x, 0.0), axis=1, keepdims=True)
        a, b, d = pick(r0, k), pick(r0, k + 1), pick(r1, k + 1)
        ra = 1.0 / a
        g = b * ra
        e = 1.0 / (d - b * g)
        ge = -g * e
        aa = ra - g * ge
        s0 = jnp.where(one_lane == k, -aa, jnp.where(one_lane == k + 1, -ge, aa * r0 + ge * r1))
        s1 = jnp.where(one_lane == k, -ge, jnp.where(one_lane == k + 1, -e, ge * r0 + e * r1))
        inside = jnp.logical_or(lane == k, lane == k + 1)
        out = jnp.where(inside, 0.0, x) - c0 * s0 - c1 * s1
        swept[...] = jnp.where(row == k, s0, jnp.where(row == k + 1, s1, out))
        return carry

    lax.fori_loop(0, NE // 2, sweep, 0)
    gains = times(-swept[...], scaled, HIGH) / NE
    seen = jnp.broadcast_to(masked, (8, MOBS))
    weights = times_t(seen, gains, HIGH)
    gain[...] = gains
    dinv_out[...] = dinv
    masked_out[...] = masked
    offset[...] = times_t(weights, ensemble[...].astype(jnp.float32), HIGH)[:1]

    fetch.wait()
    for m in range(MB):
        here = pl.ds(m * BLK, BLK)
        starts = [pl.multiple_of(pattern[0, m, k] * BLK, BLK) for k in range(KB)]
        fcols = jnp.concatenate([trans[pl.ds(s, BLK), :] for s in starts], axis=0)
        alive = active_rows[m * BLK : (m + 1) * BLK]
        forward[here, :] = times(hrows[0, here, :], fcols) * alive
    reduced[...] = times(gains, forward[...], HIGH).astype(jnp.bfloat16)


def chain_kernel(
    n, count, trans_hbm, ensemble, reduced, offset, forward, gain, member, dinv_in, masked, first,
    states, misfit,
    trans, transit, earlier, step, reduced_in,
    offset_in, step_offset, incoming, current, produced, tiles,
    trans_sem, pair_send, pair_recv, hop_send, hop_recv, tile_send, tile_recv,
):
    me = lax.axis_index("tm")
    odd = lax.rem(me, 2) == 1
    even = lax.rem(me, 2) == 0
    fetch = pltpu.make_async_copy(trans_hbm, trans, trans_sem)
    fetch.start()
    barrier = pltpu.get_barrier_semaphore()

    def greet(i, carry):
        pl.semaphore_signal(barrier, inc=1, device_id={"tm": lax.rem(me + i, n)})
        return carry

    lax.fori_loop(1, n, greet, 0)
    pl.semaphore_wait(barrier, n - 1)
    after_me = lax.rem(me + 1, n)
    after_that = lax.rem(me + 2, n)
    give_matrix = pltpu.make_async_remote_copy(
        src_ref=reduced, dst_ref=reduced_in, send_sem=pair_send.at[0], recv_sem=pair_recv.at[0],
        device_id={"tm": after_me},
    )
    give_offset = pltpu.make_async_remote_copy(
        src_ref=offset, dst_ref=offset_in, send_sem=pair_send.at[1], recv_sem=pair_recv.at[1],
        device_id={"tm": after_me},
    )
    far = pltpu.make_async_remote_copy(
        src_ref=produced, dst_ref=incoming, send_sem=hop_send.at[0], recv_sem=hop_recv,
        device_id={"tm": after_that},
    )
    near = pltpu.make_async_remote_copy(
        src_ref=produced, dst_ref=incoming, send_sem=hop_send.at[1], recv_sem=hop_recv,
        device_id={"tm": after_me},
    )

    @pl.when(even)
    def _():
        give_matrix.start()
        give_offset.start()

    fetch.wait()

    def transit_of(low_rank):
        return (trans[...].astype(jnp.float32) - times(ensemble[...], low_rank)).astype(jnp.bfloat16)

    @pl.when(even)
    def _():
        def turned(i, carry):
            here = pl.ds(pl.multiple_of(i * 256, 256), 256)
            block = trans[here, :].astype(jnp.float32) - times(ensemble[here, :], reduced[...])
            step[:, here] = block.T.astype(jnp.bfloat16)
            return carry

        lax.fori_loop(0, N // 256, turned, 0)
        step_offset[...] = offset[...]

    @pl.when(odd)
    def _():
        transit[...] = transit_of(reduced[...])
        give_matrix.wait_recv()
        give_offset.wait_recv()
        earlier[...] = transit_of(reduced_in[...])

        def product(i, carry):
            columns = pl.ds(pl.multiple_of(i * 256, 256), 256)
            step[columns, :] = times(transit[...], earlier[:, columns]).T.astype(jnp.bfloat16)
            return carry

        lax.fori_loop(0, N // 256, product, 0)
        step_offset[...] = apply_rows(transit[...], offset_in[...]) + offset[...]

    @pl.when(me < 2)
    def _():
        current[...] = first[...]

    @pl.when(me >= 2)
    def _():
        near.wait_recv()
        current[...] = incoming[...]

    parts = times(split_rows(current[...]), step[...])
    produced[...] = jnp.sum(parts, axis=0, keepdims=True) + step_offset[...]
    sends = jnp.logical_and(odd, me < n - 1)

    @pl.when(sends)
    def _():
        far.start()
        near.start()

    states[...] = produced[...]

    @pl.when(odd)
    def _():
        current[...] = apply_rows(earlier[...], current[...]) + offset_in[...]

    seen = jnp.broadcast_to(masked[...], (8, MOBS))
    innovation = seen - times_t(jnp.broadcast_to(current[...], (8, N)), forward[...], HIGH)
    moved = times_t(innovation, gain[...], HIGH)
    left = innovation - times_t(moved, member[...], HIGH)
    fit = jnp.sum(left * left * dinv_in[...], axis=1, keepdims=True) + NE * jnp.sum(
        moved * moved, axis=1, keepdims=True
    )
    tile_lane = lax.broadcasted_iota(jnp.int32, (8, NE), 1)
    tiles[me] = jnp.where(tile_lane == 0, fit, count[0].astype(jnp.float32))

    def tell(i):
        return pltpu.make_async_remote_copy(
            src_ref=tiles.at[me],
            dst_ref=tiles.at[me],
            send_sem=tile_send.at[i],
            recv_sem=tile_recv.at[me],
            device_id={"tm": lax.rem(me + i, n)},
        )

    def hear(i):
        other = lax.rem(me + n - i, n)
        return pltpu.make_async_remote_copy(
            src_ref=tiles.at[other],
            dst_ref=tiles.at[other],
            send_sem=tile_send.at[i],
            recv_sem=tile_recv.at[other],
            device_id={"tm": other},
        )

    def start(i, carry):
        tell(i).start()
        return carry

    def finish(i, carry):
        hear(i).wait_recv()
        return carry

    def sent(i, carry):
        tell(i).wait_send()
        return carry

    lax.fori_loop(1, n, start, 0)
    lax.fori_loop(1, n, finish, 0)
    lax.fori_loop(1, n, sent, 0)

    @pl.when(even)
    def _():
        give_matrix.wait_send()
        give_offset.wait_send()

    @pl.when(sends)
    def _():
        far.wait_send()
        near.wait_send()

    total = jnp.sum(tiles[...], axis=0)[:1]
    one = lax.broadcasted_iota(jnp.int32, (1, NE), 1)
    fits = jnp.sum(jnp.where(one == 0, total, 0.0), axis=1, keepdims=True)
    lives = jnp.sum(jnp.where(one == 1, total, 0.0), axis=1, keepdims=True)
    misfit[...] = jnp.broadcast_to(fits / lives, (1, NE))


def shards(
    n, trans_matrix, ensemble, obs_operator, pattern, counts, observations, obs_variance, initial_state
):
    f32, bf16 = jnp.float32, jnp.bfloat16
    hbm = pl.BlockSpec(memory_space=pltpu.HBM)
    observed = pl.pallas_call(
        observe_kernel,
        out_shape=(
            jax.ShapeDtypeStruct((NE, N), bf16),
            jax.ShapeDtypeStruct((1, N), f32),
            jax.ShapeDtypeStruct((MOBS, N), f32),
            jax.ShapeDtypeStruct((NE, MOBS), f32),
            jax.ShapeDtypeStruct((MOBS, NE), f32),
            jax.ShapeDtypeStruct((1, MOBS), f32),
            jax.ShapeDtypeStruct((1, MOBS), f32),
        ),
        in_specs=[SMEM, SMEM, hbm] + [VMEM] * 4,
        out_specs=(VMEM,) * 7,
        scratch_shapes=[
            pltpu.VMEM((N, N), bf16),
            pltpu.VMEM((NE, NE), f32),
            pltpu.SemaphoreType.DMA,
        ],
        compiler_params=pltpu.CompilerParams(vmem_limit_bytes=32 * 1024 * 1024),
        name="observe",
    )(pattern, counts, trans_matrix, ensemble, obs_operator, observations, obs_variance)
    states, misfit = pl.pallas_call(
        functools.partial(chain_kernel, n),
        out_shape=(jax.ShapeDtypeStruct((1, N), f32), jax.ShapeDtypeStruct((1, NE), f32)),
        in_specs=[SMEM, hbm] + [VMEM] * 9,
        out_specs=(VMEM, VMEM),
        scratch_shapes=[
            pltpu.VMEM((N, N), bf16),
            pltpu.VMEM((N, N), bf16),
            pltpu.VMEM((N, N), bf16),
            pltpu.VMEM((N, N), bf16),
            pltpu.VMEM((NE, N), bf16),
            pltpu.VMEM((1, N), f32),
            pltpu.VMEM((1, N), f32),
            pltpu.VMEM((1, N), f32),
            pltpu.VMEM((1, N), f32),
            pltpu.VMEM((1, N), f32),
            pltpu.VMEM((n, 8, NE), f32),
            pltpu.SemaphoreType.DMA,
            pltpu.SemaphoreType.DMA((2,)),
            pltpu.SemaphoreType.DMA((2,)),
            pltpu.SemaphoreType.DMA((2,)),
            pltpu.SemaphoreType.DMA,
            pltpu.SemaphoreType.DMA((n,)),
            pltpu.SemaphoreType.DMA((n,)),
        ],
        compiler_params=pltpu.CompilerParams(
            collective_id=0, has_side_effects=True, vmem_limit_bytes=40 * 1024 * 1024
        ),
        name="chain",
    )(counts, trans_matrix, ensemble, *observed, initial_state.reshape(1, N))
    return states, misfit[0, :1]


def solution(mesh):
    return jax.shard_map(
        functools.partial(shards, mesh.shape["tm"]),
        mesh=mesh,
        in_specs=(
            P(),
            P(),
            P(("groups", "tm"), None, None),
            P(("groups", "tm"), None, None),
            P(("groups", "tm")),
            P(("groups", "tm"), None),
            P(("groups", "tm"), None),
            P("groups"),
        ),
        out_specs=(P(("groups", "tm"), None), P("groups")),
        check_vma=False,
    )
```

```python
import functools

import jax
import jax.numpy as jnp
from jax import lax
from jax.experimental import pallas as pl
from jax.experimental.pallas import tpu as pltpu
from jax.sharding import PartitionSpec as P

N = 1024
BLK = 128
NB = 8
MB = 2
KB = 2
MOBS = 256
NE = 128
HIGH = lax.Precision.HIGHEST
VMEM = pl.BlockSpec(memory_space=pltpu.VMEM)
SMEM = pl.BlockSpec(memory_space=pltpu.SMEM)


def times(left, right, precision=None):
    return lax.dot_general(
        left, right, (((1,), (0,)), ((), ())), precision=precision, preferred_element_type=jnp.float32
    )


def times_t(left, right, precision=None):
    return lax.dot_general(
        left, right, (((1,), (1,)), ((), ())), precision=precision, preferred_element_type=jnp.float32
    )


def split_rows(vector):
    high = vector.astype(jnp.bfloat16).astype(jnp.float32)
    rest = vector - high
    middle = rest.astype(jnp.bfloat16).astype(jnp.float32)
    lowest = rest - middle
    row = lax.broadcasted_iota(jnp.int32, (16, N), 0)
    stacked = jnp.where(row == 0, high, jnp.where(row == 1, middle, jnp.where(row == 2, lowest, 0.0)))
    return stacked.astype(jnp.bfloat16)


def apply_rows(matrix, vector):
    return jnp.sum(times_t(split_rows(vector), matrix), axis=0, keepdims=True)


def observe_kernel(
    pattern, count, trans_hbm, ensemble, hrows, yobs, rvar,
    reduced, offset, forward, gain, member, dinv_out, masked_out,
    trans, swept, trans_sem,
):
    fetch = pltpu.make_async_copy(trans_hbm, trans, trans_sem)
    fetch.start()
    live = count[0]
    rows = lax.broadcasted_iota(jnp.int32, (MOBS, 1), 0)
    active_rows = (rows < live).astype(jnp.float32)
    lanes = lax.broadcasted_iota(jnp.int32, (1, MOBS), 1)
    active_lanes = (lanes < live).astype(jnp.float32)
    for m in range(MB):
        here = pl.ds(m * BLK, BLK)
        starts = [pl.multiple_of(pattern[0, m, k] * BLK, BLK) for k in range(KB)]
        ecols = jnp.concatenate([ensemble[pl.ds(s, BLK), :] for s in starts], axis=0)
        alive = active_rows[m * BLK : (m + 1) * BLK]
        member[here, :] = times(hrows[0, here, :], ecols) * alive
    dinv = active_lanes / rvar[...]
    masked = yobs[...] * active_lanes
    scaled = member[...].T * dinv
    row = lax.broadcasted_iota(jnp.int32, (NE, NE), 0)
    lane = lax.broadcasted_iota(jnp.int32, (NE, NE), 1)
    begin = times(scaled, member[...], HIGH) / NE + (row == lane).astype(jnp.float32)
    swept[...] = (begin + begin.T) * 0.5

    one_lane = lax.broadcasted_iota(jnp.int32, (1, NE), 1)

    def pick(vector, k):
        return jnp.sum(jnp.where(one_lane == k, vector, 0.0), axis=1, keepdims=True)

    def sweep(j, carry):
        k = 2 * j
        x = swept[...]
        r0 = swept[pl.ds(k, 1), :]
        r1 = swept[pl.ds(k + 1, 1), :]
        c0 = jnp.sum(jnp.where(lane == k, x, 0.0), axis=1, keepdims=True)
        c1 = jnp.sum(jnp.where(lane == k + 1, x, 0.0), axis=1, keepdims=True)
        a, b, d = pick(r0, k), pick(r0, k + 1), pick(r1, k + 1)
        ra = 1.0 / a
        g = b * ra
        e = 1.0 / (d - b * g)
        ge = -g * e
        aa = ra - g * ge
        s0 = jnp.where(one_lane == k, -aa, jnp.where(one_lane == k + 1, -ge, aa * r0 + ge * r1))
        s1 = jnp.where(one_lane == k, -ge, jnp.where(one_lane == k + 1, -e, ge * r0 + e * r1))
        inside = jnp.logical_or(lane == k, lane == k + 1)
        out = jnp.where(inside, 0.0, x) - c0 * s0 - c1 * s1
        swept[...] = jnp.where(row == k, s0, jnp.where(row == k + 1, s1, out))
        return carry

    lax.fori_loop(0, NE // 2, sweep, 0)
    gains = times(-swept[...], scaled, HIGH) / NE
    seen = jnp.broadcast_to(masked, (8, MOBS))
    weights = times_t(seen, gains, HIGH)
    gain[...] = gains
    dinv_out[...] = dinv
    masked_out[...] = masked
    offset[...] = times_t(weights, ensemble[...].astype(jnp.float32), HIGH)[:1]

    fetch.wait()
    for m in range(MB):
        here = pl.ds(m * BLK, BLK)
        starts = [pl.multiple_of(pattern[0, m, k] * BLK, BLK) for k in range(KB)]
        fcols = jnp.concatenate([trans[pl.ds(s, BLK), :] for s in starts], axis=0)
        alive = active_rows[m * BLK : (m + 1) * BLK]
        forward[here, :] = times(hrows[0, here, :], fcols) * alive
    reduced[...] = times(gains, forward[...], HIGH).astype(jnp.bfloat16)


def chain_kernel(
    n, count, trans_hbm, ensemble, reduced, offset, forward, gain, member, dinv_in, masked, first,
    states, misfit,
    trans, transit, earlier, step, reduced_in,
    offset_in, step_offset, incoming, current, produced, tiles,
    trans_sem, pair_send, pair_recv, hop_send, hop_recv, tile_send, tile_recv,
):
    me = lax.axis_index("tm")
    odd = lax.rem(me, 2) == 1
    even = lax.rem(me, 2) == 0
    in_turn = jnp.logical_and(odd, me < 4)
    composed = jnp.logical_and(odd, me >= 4)
    fetch = pltpu.make_async_copy(trans_hbm, trans, trans_sem)
    fetch.start()
    barrier = pltpu.get_barrier_semaphore()

    def greet(i, carry):
        pl.semaphore_signal(barrier, inc=1, device_id={"tm": lax.rem(me + i, n)})
        return carry

    lax.fori_loop(1, n, greet, 0)
    pl.semaphore_wait(barrier, n - 1)
    after_me = lax.rem(me + 1, n)
    after_that = lax.rem(me + 2, n)
    give_matrix = pltpu.make_async_remote_copy(
        src_ref=reduced, dst_ref=reduced_in, send_sem=pair_send.at[0], recv_sem=pair_recv.at[0],
        device_id={"tm": after_me},
    )
    give_offset = pltpu.make_async_remote_copy(
        src_ref=offset, dst_ref=offset_in, send_sem=pair_send.at[1], recv_sem=pair_recv.at[1],
        device_id={"tm": after_me},
    )
    far = pltpu.make_async_remote_copy(
        src_ref=produced, dst_ref=incoming, send_sem=hop_send.at[0], recv_sem=hop_recv,
        device_id={"tm": after_that},
    )
    near = pltpu.make_async_remote_copy(
        src_ref=produced, dst_ref=incoming, send_sem=hop_send.at[1], recv_sem=hop_recv,
        device_id={"tm": after_me},
    )

    @pl.when(even)
    def _():
        give_matrix.start()
        give_offset.start()

    fetch.wait()

    def transit_of(low_rank):
        return (trans[...].astype(jnp.float32) - times(ensemble[...], low_rank)).astype(jnp.bfloat16)

    @pl.when(even)
    def _():
        def turned(i, carry):
            here = pl.ds(pl.multiple_of(i * 256, 256), 256)
            block = trans[here, :].astype(jnp.float32) - times(ensemble[here, :], reduced[...])
            step[:, here] = block.T.astype(jnp.bfloat16)
            return carry

        lax.fori_loop(0, N // 256, turned, 0)
        step_offset[...] = offset[...]

    @pl.when(odd)
    def _():
        transit[...] = transit_of(reduced[...])
        give_matrix.wait_recv()
        give_offset.wait_recv()
        earlier[...] = transit_of(reduced_in[...])

    @pl.when(composed)
    def _():
        def product(i, carry):
            columns = pl.ds(pl.multiple_of(i * 256, 256), 256)
            step[columns, :] = times(transit[...], earlier[:, columns]).T.astype(jnp.bfloat16)
            return carry

        lax.fori_loop(0, N // 256, product, 0)
        step_offset[...] = apply_rows(transit[...], offset_in[...]) + offset[...]

    @pl.when(me < 2)
    def _():
        current[...] = first[...]

    @pl.when(me >= 2)
    def _():
        near.wait_recv()
        current[...] = incoming[...]

    @pl.when(in_turn)
    def _():
        between = apply_rows(earlier[...], current[...]) + offset_in[...]
        produced[...] = apply_rows(transit[...], between) + offset[...]

    @pl.when(jnp.logical_or(even, composed))
    def _():
        parts = times(split_rows(current[...]), step[...])
        produced[...] = jnp.sum(parts, axis=0, keepdims=True) + step_offset[...]

    sends = jnp.logical_and(odd, me < n - 1)

    @pl.when(sends)
    def _():
        far.start()
        near.start()

    states[...] = produced[...]

    @pl.when(odd)
    def _():
        current[...] = apply_rows(earlier[...], current[...]) + offset_in[...]

    seen = jnp.broadcast_to(masked[...], (8, MOBS))
    innovation = seen - times_t(jnp.broadcast_to(current[...], (8, N)), forward[...], HIGH)
    moved = times_t(innovation, gain[...], HIGH)
    left = innovation - times_t(moved, member[...], HIGH)
    fit = jnp.sum(left * left * dinv_in[...], axis=1, keepdims=True) + NE * jnp.sum(
        moved * moved, axis=1, keepdims=True
    )
    tile_lane = lax.broadcasted_iota(jnp.int32, (8, NE), 1)
    tiles[me] = jnp.where(tile_lane == 0, fit, count[0].astype(jnp.float32))

    def tell(i):
        return pltpu.make_async_remote_copy(
            src_ref=tiles.at[me],
            dst_ref=tiles.at[me],
            send_sem=tile_send.at[i],
            recv_sem=tile_recv.at[me],
            device_id={"tm": lax.rem(me + i, n)},
        )

    def hear(i):
        other = lax.rem(me + n - i, n)
        return pltpu.make_async_remote_copy(
            src_ref=tiles.at[other],
            dst_ref=tiles.at[other],
            send_sem=tile_send.at[i],
            recv_sem=tile_recv.at[other],
            device_id={"tm": other},
        )

    def start(i, carry):
        tell(i).start()
        return carry

    def finish(i, carry):
        hear(i).wait_recv()
        return carry

    def sent(i, carry):
        tell(i).wait_send()
        return carry

    lax.fori_loop(1, n, start, 0)
    lax.fori_loop(1, n, finish, 0)
    lax.fori_loop(1, n, sent, 0)

    @pl.when(even)
    def _():
        give_matrix.wait_send()
        give_offset.wait_send()

    @pl.when(sends)
    def _():
        far.wait_send()
        near.wait_send()

    total = jnp.sum(tiles[...], axis=0)[:1]
    one = lax.broadcasted_iota(jnp.int32, (1, NE), 1)
    fits = jnp.sum(jnp.where(one == 0, total, 0.0), axis=1, keepdims=True)
    lives = jnp.sum(jnp.where(one == 1, total, 0.0), axis=1, keepdims=True)
    misfit[...] = jnp.broadcast_to(fits / lives, (1, NE))


def shards(
    n, trans_matrix, ensemble, obs_operator, pattern, counts, observations, obs_variance, initial_state
):
    f32, bf16 = jnp.float32, jnp.bfloat16
    hbm = pl.BlockSpec(memory_space=pltpu.HBM)
    observed = pl.pallas_call(
        observe_kernel,
        out_shape=(
            jax.ShapeDtypeStruct((NE, N), bf16),
            jax.ShapeDtypeStruct((1, N), f32),
            jax.ShapeDtypeStruct((MOBS, N), f32),
            jax.ShapeDtypeStruct((NE, MOBS), f32),
            jax.ShapeDtypeStruct((MOBS, NE), f32),
            jax.ShapeDtypeStruct((1, MOBS), f32),
            jax.ShapeDtypeStruct((1, MOBS), f32),
        ),
        in_specs=[SMEM, SMEM, hbm] + [VMEM] * 4,
        out_specs=(VMEM,) * 7,
        scratch_shapes=[
            pltpu.VMEM((N, N), bf16),
            pltpu.VMEM((NE, NE), f32),
            pltpu.SemaphoreType.DMA,
        ],
        compiler_params=pltpu.CompilerParams(vmem_limit_bytes=32 * 1024 * 1024),
        name="observe",
    )(pattern, counts, trans_matrix, ensemble, obs_operator, observations, obs_variance)
    states, misfit = pl.pallas_call(
        functools.partial(chain_kernel, n),
        out_shape=(jax.ShapeDtypeStruct((1, N), f32), jax.ShapeDtypeStruct((1, NE), f32)),
        in_specs=[SMEM, hbm] + [VMEM] * 9,
        out_specs=(VMEM, VMEM),
        scratch_shapes=[
            pltpu.VMEM((N, N), bf16),
            pltpu.VMEM((N, N), bf16),
            pltpu.VMEM((N, N), bf16),
            pltpu.VMEM((N, N), bf16),
            pltpu.VMEM((NE, N), bf16),
            pltpu.VMEM((1, N), f32),
            pltpu.VMEM((1, N), f32),
            pltpu.VMEM((1, N), f32),
            pltpu.VMEM((1, N), f32),
            pltpu.VMEM((1, N), f32),
            pltpu.VMEM((n, 8, NE), f32),
            pltpu.SemaphoreType.DMA,
            pltpu.SemaphoreType.DMA((2,)),
            pltpu.SemaphoreType.DMA((2,)),
            pltpu.SemaphoreType.DMA((2,)),
            pltpu.SemaphoreType.DMA,
            pltpu.SemaphoreType.DMA((n,)),
            pltpu.SemaphoreType.DMA((n,)),
        ],
        compiler_params=pltpu.CompilerParams(
            collective_id=0, has_side_effects=True, vmem_limit_bytes=40 * 1024 * 1024
        ),
        name="chain",
    )(counts, trans_matrix, ensemble, *observed, initial_state.reshape(1, N))
    return states, misfit[0, :1]


def solution(mesh):
    return jax.shard_map(
        functools.partial(shards, mesh.shape["tm"]),
        mesh=mesh,
        in_specs=(
            P(),
            P(),
            P(("groups", "tm"), None, None),
            P(("groups", "tm"), None, None),
            P(("groups", "tm")),
            P(("groups", "tm"), None),
            P(("groups", "tm"), None),
            P("groups"),
        ),
        out_specs=(P(("groups", "tm"), None), P("groups")),
        check_vma=False,
    )
```

```python
import functools

import jax
import jax.numpy as jnp
from jax import lax
from jax.experimental import pallas as pl
from jax.experimental.pallas import tpu as pltpu
from jax.sharding import PartitionSpec as P

N = 1024
BLK = 128
NB = 8
MB = 2
KB = 2
MOBS = 256
NE = 128
HIGH = lax.Precision.HIGHEST
VMEM = pl.BlockSpec(memory_space=pltpu.VMEM)
SMEM = pl.BlockSpec(memory_space=pltpu.SMEM)


def times(left, right, precision=None):
    return lax.dot_general(
        left, right, (((1,), (0,)), ((), ())), precision=precision, preferred_element_type=jnp.float32
    )


def times_t(left, right, precision=None):
    return lax.dot_general(
        left, right, (((1,), (1,)), ((), ())), precision=precision, preferred_element_type=jnp.float32
    )


def split_rows(vector):
    high = vector.astype(jnp.bfloat16).astype(jnp.float32)
    rest = vector - high
    middle = rest.astype(jnp.bfloat16).astype(jnp.float32)
    lowest = rest - middle
    row = lax.broadcasted_iota(jnp.int32, (16, N), 0)
    stacked = jnp.where(row == 0, high, jnp.where(row == 1, middle, jnp.where(row == 2, lowest, 0.0)))
    return stacked.astype(jnp.bfloat16)


def apply_rows(matrix, vector):
    return jnp.sum(times_t(split_rows(vector), matrix), axis=0, keepdims=True)


def observe_kernel(
    pattern, count, trans_hbm, ensemble, hrows, yobs, rvar,
    reduced, offset, forward, gain, member, dinv_out, masked_out,
    trans, swept, trans_sem,
):
    fetch = pltpu.make_async_copy(trans_hbm, trans, trans_sem)
    fetch.start()
    live = count[0]
    rows = lax.broadcasted_iota(jnp.int32, (MOBS, 1), 0)
    active_rows = (rows < live).astype(jnp.float32)
    lanes = lax.broadcasted_iota(jnp.int32, (1, MOBS), 1)
    active_lanes = (lanes < live).astype(jnp.float32)
    for m in range(MB):
        here = pl.ds(m * BLK, BLK)
        starts = [pl.multiple_of(pattern[0, m, k] * BLK, BLK) for k in range(KB)]
        ecols = jnp.concatenate([ensemble[pl.ds(s, BLK), :] for s in starts], axis=0)
        alive = active_rows[m * BLK : (m + 1) * BLK]
        member[here, :] = times(hrows[0, here, :], ecols) * alive
    dinv = active_lanes / rvar[...]
    masked = yobs[...] * active_lanes
    scaled = member[...].T * dinv
    row = lax.broadcasted_iota(jnp.int32, (NE, NE), 0)
    lane = lax.broadcasted_iota(jnp.int32, (NE, NE), 1)
    begin = times(scaled, member[...], HIGH) / NE + (row == lane).astype(jnp.float32)
    swept[...] = (begin + begin.T) * 0.5

    one_lane = lax.broadcasted_iota(jnp.int32, (1, NE), 1)

    def pick(vector, k):
        return jnp.sum(jnp.where(one_lane == k, vector, 0.0), axis=1, keepdims=True)

    def sweep(j, carry):
        k = 2 * j
        x = swept[...]
        r0 = swept[pl.ds(k, 1), :]
        r1 = swept[pl.ds(k + 1, 1), :]
        c0 = jnp.sum(jnp.where(lane == k, x, 0.0), axis=1, keepdims=True)
        c1 = jnp.sum(jnp.where(lane == k + 1, x, 0.0), axis=1, keepdims=True)
        a, b, d = pick(r0, k), pick(r0, k + 1), pick(r1, k + 1)
        ra = 1.0 / a
        g = b * ra
        e = 1.0 / (d - b * g)
        ge = -g * e
        aa = ra - g * ge
        s0 = jnp.where(one_lane == k, -aa, jnp.where(one_lane == k + 1, -ge, aa * r0 + ge * r1))
        s1 = jnp.where(one_lane == k, -ge, jnp.where(one_lane == k + 1, -e, ge * r0 + e * r1))
        inside = jnp.logical_or(lane == k, lane == k + 1)
        out = jnp.where(inside, 0.0, x) - c0 * s0 - c1 * s1
        swept[...] = jnp.where(row == k, s0, jnp.where(row == k + 1, s1, out))
        return carry

    lax.fori_loop(0, NE // 2, sweep, 0)
    gains = times(-swept[...], scaled, HIGH) / NE
    seen = jnp.broadcast_to(masked, (8, MOBS))
    weights = times_t(seen, gains, HIGH)
    gain[...] = gains
    dinv_out[...] = dinv
    masked_out[...] = masked
    offset[...] = times_t(weights, ensemble[...].astype(jnp.float32), HIGH)[:1]

    fetch.wait()
    for m in range(MB):
        here = pl.ds(m * BLK, BLK)
        starts = [pl.multiple_of(pattern[0, m, k] * BLK, BLK) for k in range(KB)]
        fcols = jnp.concatenate([trans[pl.ds(s, BLK), :] for s in starts], axis=0)
        alive = active_rows[m * BLK : (m + 1) * BLK]
        forward[here, :] = times(hrows[0, here, :], fcols) * alive
    reduced[...] = times(gains, forward[...], HIGH).astype(jnp.bfloat16)


def chain_kernel(
    n, count, trans_hbm, ensemble, reduced, offset, forward, gain, member, dinv_in, masked, first,
    states, misfit,
    trans, transit, earlier, step, reduced_in,
    offset_in, step_offset, incoming, current, produced, tiles,
    trans_sem, pair_send, pair_recv, hop_send, hop_recv, tile_send, tile_recv,
):
    me = lax.axis_index("tm")
    odd = lax.rem(me, 2) == 1
    even = lax.rem(me, 2) == 0
    sends = jnp.logical_and(odd, me < n - 1)
    in_turn = jnp.logical_and(sends, me < 4)
    composed = jnp.logical_and(sends, me >= 4)
    fetch = pltpu.make_async_copy(trans_hbm, trans, trans_sem)
    fetch.start()
    barrier = pltpu.get_barrier_semaphore()

    def greet(i, carry):
        pl.semaphore_signal(barrier, inc=1, device_id={"tm": lax.rem(me + i, n)})
        return carry

    lax.fori_loop(1, n, greet, 0)
    pl.semaphore_wait(barrier, n - 1)
    after_me = lax.rem(me + 1, n)
    after_that = lax.rem(me + 2, n)
    give_matrix = pltpu.make_async_remote_copy(
        src_ref=reduced, dst_ref=reduced_in, send_sem=pair_send.at[0], recv_sem=pair_recv.at[0],
        device_id={"tm": after_me},
    )
    give_offset = pltpu.make_async_remote_copy(
        src_ref=offset, dst_ref=offset_in, send_sem=pair_send.at[1], recv_sem=pair_recv.at[1],
        device_id={"tm": after_me},
    )
    far = pltpu.make_async_remote_copy(
        src_ref=produced, dst_ref=incoming, send_sem=hop_send.at[0], recv_sem=hop_recv,
        device_id={"tm": after_that},
    )
    near = pltpu.make_async_remote_copy(
        src_ref=produced, dst_ref=incoming, send_sem=hop_send.at[1], recv_sem=hop_recv,
        device_id={"tm": after_me},
    )

    @pl.when(even)
    def _():
        give_matrix.start()
        give_offset.start()

    fetch.wait()

    def transit_of(low_rank):
        return (trans[...].astype(jnp.float32) - times(ensemble[...], low_rank)).astype(jnp.bfloat16)

    @pl.when(even)
    def _():
        def turned(i, carry):
            here = pl.ds(pl.multiple_of(i * 256, 256), 256)
            block = trans[here, :].astype(jnp.float32) - times(ensemble[here, :], reduced[...])
            step[:, here] = block.T.astype(jnp.bfloat16)
            return carry

        lax.fori_loop(0, N // 256, turned, 0)
        step_offset[...] = offset[...]

    @pl.when(odd)
    def _():
        transit[...] = transit_of(reduced[...])
        give_matrix.wait_recv()
        give_offset.wait_recv()
        earlier[...] = transit_of(reduced_in[...])

    @pl.when(composed)
    def _():
        def product(i, carry):
            columns = pl.ds(pl.multiple_of(i * 256, 256), 256)
            step[columns, :] = times(transit[...], earlier[:, columns]).T.astype(jnp.bfloat16)
            return carry

        lax.fori_loop(0, N // 256, product, 0)
        step_offset[...] = apply_rows(transit[...], offset_in[...]) + offset[...]

    @pl.when(me < 2)
    def _():
        current[...] = first[...]

    @pl.when(me >= 2)
    def _():
        near.wait_recv()
        current[...] = incoming[...]

    @pl.when(in_turn)
    def _():
        between = apply_rows(earlier[...], current[...]) + offset_in[...]
        produced[...] = apply_rows(transit[...], between) + offset[...]

    @pl.when(composed)
    def _():
        parts = times(split_rows(current[...]), step[...])
        produced[...] = jnp.sum(parts, axis=0, keepdims=True) + step_offset[...]

    @pl.when(sends)
    def _():
        far.start()
        near.start()

    @pl.when(odd)
    def _():
        current[...] = apply_rows(earlier[...], current[...]) + offset_in[...]

    seen = jnp.broadcast_to(masked[...], (8, MOBS))
    innovation = seen - times_t(jnp.broadcast_to(current[...], (8, N)), forward[...], HIGH)
    moved = times_t(innovation, gain[...], HIGH)
    left = innovation - times_t(moved, member[...], HIGH)
    fit = jnp.sum(left * left * dinv_in[...], axis=1, keepdims=True) + NE * jnp.sum(
        moved * moved, axis=1, keepdims=True
    )
    tile_lane = lax.broadcasted_iota(jnp.int32, (8, NE), 1)
    tiles[me] = jnp.where(tile_lane == 0, fit, count[0].astype(jnp.float32))

    def tell(i):
        return pltpu.make_async_remote_copy(
            src_ref=tiles.at[me],
            dst_ref=tiles.at[me],
            send_sem=tile_send.at[i],
            recv_sem=tile_recv.at[me],
            device_id={"tm": lax.rem(me + i, n)},
        )

    def hear(i):
        other = lax.rem(me + n - i, n)
        return pltpu.make_async_remote_copy(
            src_ref=tiles.at[other],
            dst_ref=tiles.at[other],
            send_sem=tile_send.at[i],
            recv_sem=tile_recv.at[other],
            device_id={"tm": other},
        )

    def start(i, carry):
        tell(i).start()
        return carry

    def finish(i, carry):
        hear(i).wait_recv()
        return carry

    def sent(i, carry):
        tell(i).wait_send()
        return carry

    lax.fori_loop(1, n, start, 0)

    @pl.when(even)
    def _():
        parts = times(split_rows(current[...]), step[...])
        produced[...] = jnp.sum(parts, axis=0, keepdims=True) + step_offset[...]

    @pl.when(me == n - 1)
    def _():
        produced[...] = apply_rows(transit[...], current[...]) + offset[...]

    states[...] = produced[...]
    lax.fori_loop(1, n, finish, 0)
    lax.fori_loop(1, n, sent, 0)

    @pl.when(even)
    def _():
        give_matrix.wait_send()
        give_offset.wait_send()

    @pl.when(sends)
    def _():
        far.wait_send()
        near.wait_send()

    total = jnp.sum(tiles[...], axis=0)[:1]
    one = lax.broadcasted_iota(jnp.int32, (1, NE), 1)
    fits = jnp.sum(jnp.where(one == 0, total, 0.0), axis=1, keepdims=True)
    lives = jnp.sum(jnp.where(one == 1, total, 0.0), axis=1, keepdims=True)
    misfit[...] = jnp.broadcast_to(fits / lives, (1, NE))


def shards(
    n, trans_matrix, ensemble, obs_operator, pattern, counts, observations, obs_variance, initial_state
):
    f32, bf16 = jnp.float32, jnp.bfloat16
    hbm = pl.BlockSpec(memory_space=pltpu.HBM)
    observed = pl.pallas_call(
        observe_kernel,
        out_shape=(
            jax.ShapeDtypeStruct((NE, N), bf16),
            jax.ShapeDtypeStruct((1, N), f32),
            jax.ShapeDtypeStruct((MOBS, N), f32),
            jax.ShapeDtypeStruct((NE, MOBS), f32),
            jax.ShapeDtypeStruct((MOBS, NE), f32),
            jax.ShapeDtypeStruct((1, MOBS), f32),
            jax.ShapeDtypeStruct((1, MOBS), f32),
        ),
        in_specs=[SMEM, SMEM, hbm] + [VMEM] * 4,
        out_specs=(VMEM,) * 7,
        scratch_shapes=[
            pltpu.VMEM((N, N), bf16),
            pltpu.VMEM((NE, NE), f32),
            pltpu.SemaphoreType.DMA,
        ],
        compiler_params=pltpu.CompilerParams(vmem_limit_bytes=32 * 1024 * 1024),
        name="observe",
    )(pattern, counts, trans_matrix, ensemble, obs_operator, observations, obs_variance)
    states, misfit = pl.pallas_call(
        functools.partial(chain_kernel, n),
        out_shape=(jax.ShapeDtypeStruct((1, N), f32), jax.ShapeDtypeStruct((1, NE), f32)),
        in_specs=[SMEM, hbm] + [VMEM] * 9,
        out_specs=(VMEM, VMEM),
        scratch_shapes=[
            pltpu.VMEM((N, N), bf16),
            pltpu.VMEM((N, N), bf16),
            pltpu.VMEM((N, N), bf16),
            pltpu.VMEM((N, N), bf16),
            pltpu.VMEM((NE, N), bf16),
            pltpu.VMEM((1, N), f32),
            pltpu.VMEM((1, N), f32),
            pltpu.VMEM((1, N), f32),
            pltpu.VMEM((1, N), f32),
            pltpu.VMEM((1, N), f32),
            pltpu.VMEM((n, 8, NE), f32),
            pltpu.SemaphoreType.DMA,
            pltpu.SemaphoreType.DMA((2,)),
            pltpu.SemaphoreType.DMA((2,)),
            pltpu.SemaphoreType.DMA((2,)),
            pltpu.SemaphoreType.DMA,
            pltpu.SemaphoreType.DMA((n,)),
            pltpu.SemaphoreType.DMA((n,)),
        ],
        compiler_params=pltpu.CompilerParams(
            collective_id=0, has_side_effects=True, vmem_limit_bytes=40 * 1024 * 1024
        ),
        name="chain",
    )(counts, trans_matrix, ensemble, *observed, initial_state.reshape(1, N))
    return states, misfit[0, :1]


def solution(mesh):
    return jax.shard_map(
        functools.partial(shards, mesh.shape["tm"]),
        mesh=mesh,
        in_specs=(
            P(),
            P(),
            P(("groups", "tm"), None, None),
            P(("groups", "tm"), None, None),
            P(("groups", "tm")),
            P(("groups", "tm"), None),
            P(("groups", "tm"), None),
            P("groups"),
        ),
        out_specs=(P(("groups", "tm"), None), P("groups")),
        check_vma=False,
    )
```
